512 devices in a mesh: gx: 4 (over x), gy: 4 (over z_lo), gz: 32 (over z_hi, y, core).
Axes of the slice: x: 4, y: 8, z: 8 (z_hi: 2, z_lo: 4; z = z_hi * 4 + z_lo), core: 2. Of those that a mesh axis runs over, the one named last changes fastest.
Arguments:
- layer_input: bfloat16 [16, 32, 256, 128], P('gx', 'gy', 'gz'), may hold values from -6 to 6
- pre_one: bfloat16 [16, 32, 256, 128], P('gx', 'gy', 'gz'), may hold values from -6 to 6
- pre_two: bfloat16 [16, 32, 256, 128], P('gx', 'gy', 'gz'), may hold values from -6 to 6
- out_grad: bfloat16 [16, 32, 256, 128], P('gx', 'gy', 'gz'), may hold values from -6 to 6
- weight_one: bfloat16 [3, 3, 3, 128, 128], replicated, may hold values from -0.109375 to 0.109375
- weight_two: bfloat16 [3, 3, 3, 128, 128], replicated, may hold values from -0.109375 to 0.109375
Outputs:
- input_grad: bfloat16 [16, 32, 256, 128], P('gx', 'gy', 'gz')
- grad_one: bfloat16 [3, 3, 3, 128, 128], replicated
- grad_two: bfloat16 [3, 3, 3, 128, 128], replicated
The draws below stay inside these ranges and needn't reach their ends.
All inputs are finite; a program needn't handle non-finite values.
Results may differ from the reference program's by a relative error of at most 0.0053.
Values may be sent and summed in bfloat16 or wider, within the bound.
No kernel may reach another device: no remote copies, remote signals or barrier semaphores. Data moves between devices by JAX's collectives and lax.ppermute only.
A program may use at most 64 MiB of HBM per device.

```python
import jax
import jax.numpy as jnp

C = 128
NX = 16
NY = 32
NZ = 256


def spiked(values, key, source, target, shards_of, factor):
    def block_of(position):
        return (jnp.arange(values.shape[position]) // (values.shape[position] // shards_of)).reshape((-1,) + (1,) * (values.ndim - 1 - position))

    first = jax.random.permutation(key, shards_of)[block_of(target)]
    other_side = (block_of(target) + shards_of // 2) % shards_of
    return jnp.where((block_of(source) == first) | (block_of(source) == other_side), factor * values, values)


def steps_of(own_key, extent, split, smallest, high):
    factor_of, own = 1.0, jax.random.fold_in(own_key, 6)
    for dim, parts in split:
        steps = jnp.exp(jax.random.uniform(jax.random.fold_in(own, dim), (parts,), jnp.float32, smallest / len(split), high / len(split)))
        factor_of = factor_of * jnp.repeat(steps, extent[dim] // parts).reshape([-1 if axis == dim else 1 for axis in range(len(extent))])
    return factor_of


def normal_values(rng, shape, spread, bound, split=(), kind=jnp.bfloat16):
    level = steps_of(rng, shape, split, -0.22, 0.18) if split else 1.0
    drawn = jax.random.normal(rng, shape, jnp.float32) * spread * level
    return jnp.minimum(jnp.maximum(drawn, -bound), bound).astype(kind)


def gaussian_with(rng, dims, spread, most, shards, heavy, kind=jnp.bfloat16):
    values = spread * jax.random.normal(rng, dims, jnp.float32)
    if shards:
        values = values * steps_of(rng, dims, shards, -0.22, 0.18)
    return jnp.clip(spiked(values, jax.random.fold_in(rng, 3), *heavy), -most, most).astype(kind)


def setup_inputs(seed: int = 0) -> dict:
    keys = jax.random.split(jax.random.key(seed), 7)
    return {
        "layer_input": normal_values(keys[0], (NX, NY, NZ, C), 1.0, 6.0, ((0, 4), (1, 4), (2, 32))),
        "pre_one": normal_values(keys[1], (NX, NY, NZ, C), 1.0, 6.0, ((0, 4), (1, 4), (2, 32))),
        "pre_two": normal_values(keys[2], (NX, NY, NZ, C), 1.0, 6.0, ((0, 4), (1, 4), (2, 32))),
        "out_grad": gaussian_with(keys[3], (NX, NY, NZ, C), 1.0, 6.0, ((0, 4), (1, 4), (2, 32)), (2, 3, 32, 2.75)),
        "weight_one": normal_values(keys[4], (3, 3, 3, C, C), (27 * C) ** -0.5, 0.109375),
        "weight_two": normal_values(keys[5], (3, 3, 3, C, C), (27 * C) ** -0.5, 0.109375),
    }


slope_low = 0.3

def leak_slope(pre):
    return jnp.where(pre > 0, 1.0, slope_low).astype(jnp.float32)

def layer_back(act, grad, weight):
    size_x, size_y, size_z, chans = act.shape
    padded = jnp.pad(grad, ((1, 1), (1, 1), (1, 1), (0, 0)))
    acts = act.reshape(-1, chans).astype(jnp.float32)
    kernel_rows = []
    d_input = jnp.zeros((size_x * size_y * size_z, chans), jnp.float32)
    for first in range(3):
        for second in range(3):
            for third in range(3):
                window = padded[2 - first:2 - first + size_x, 2 - second:2 - second + size_y, 2 - third:2 - third + size_z]
                window = window.reshape(-1, chans).astype(jnp.float32)
                kernel_rows.append(jnp.dot(acts.T, window))
                d_input = d_input + jnp.dot(window, weight[first, second, third].astype(jnp.float32).T)
    kernel = jnp.stack(kernel_rows).reshape(3, 3, 3, chans, chans)
    return (kernel, d_input.reshape(size_x, size_y, size_z, chans))

def reference(layer_input, pre_one, pre_two, out_grad, weight_one, weight_two):
    scale = 1.0 / jnp.sqrt(jnp.float32(NX * NY * NZ))
    pre_one_f = pre_one.astype(jnp.float32)
    hidden = (pre_one_f * leak_slope(pre_one_f)).astype(jnp.bfloat16)
    g_two = (out_grad.astype(jnp.float32) * leak_slope(pre_two.astype(jnp.float32))).astype(jnp.bfloat16)
    kernel_two, d_hidden = layer_back(hidden, g_two, weight_two)
    g_one = (d_hidden * leak_slope(pre_one_f)).astype(jnp.bfloat16)
    kernel_one, d_input = layer_back(layer_input, g_one, weight_one)
    grad_two = (kernel_two * scale).astype(jnp.bfloat16)
    grad_one = (kernel_one * scale).astype(jnp.bfloat16)
    return (d_input.astype(jnp.bfloat16), grad_one, grad_two)
```

```python
import functools

import jax
import jax.numpy as jnp
from jax import lax
from jax.experimental import pallas as pl
from jax.experimental.pallas import tpu as pltpu
from jax.sharding import Mesh
from jax.sharding import PartitionSpec as P

slope_low = 0.3
Z = ("gh", "gw", "gc")
REDUCE = ("gx", "gy", "gh", "gw")
C = 128
PITCH = 16
F32 = jnp.float32
BF16 = jnp.bfloat16


def exchange(up, down, axis):
    peers = lax.axis_size(axis)
    right = [(i, i + 1) for i in range(peers - 1)]
    left = [(i + 1, i) for i in range(peers - 1)]
    return lax.ppermute(up, axis, right), lax.ppermute(down, axis, left)


def pack(g, s):
    lines = g.shape[2]
    return jnp.concatenate(
        [g.reshape(-1, lines, C), s.reshape(-1, lines, C)], axis=0
    )


def unpack(rows, g_shape, s_shape):
    n = g_shape[0] * g_shape[1]
    return rows[:n].reshape(g_shape), rows[n:].reshape(s_shape)


def extend(g, s):
    nx, ny, nz, _ = g.shape
    up, down = exchange(pack(g[-2:], s[-1:]), pack(g[:2], s[:1]), "gx")
    shapes = ((2, ny, nz, C), (1, ny, nz, C))
    (g_lo, s_lo), (g_hi, s_hi) = unpack(up, *shapes), unpack(down, *shapes)
    g = jnp.concatenate([g_lo, g, g_hi], axis=0)
    s = jnp.concatenate([s_lo, s, s_hi], axis=0)

    up, down = exchange(
        pack(g[:, -2:], s[:, -1:]), pack(g[:, :2], s[:, :1]), "gy"
    )
    shapes = ((nx + 4, 2, nz, C), (nx + 2, 1, nz, C))
    (g_lo, s_lo), (g_hi, s_hi) = unpack(up, *shapes), unpack(down, *shapes)
    g = jnp.concatenate([g_lo, g, g_hi], axis=1)
    s = jnp.concatenate([s_lo, s, s_hi], axis=1)

    def flat(g_face, s_face):
        return jnp.concatenate(
            [g_face.reshape(-1, C), s_face.reshape(-1, C)], axis=0
        )

    up, down = exchange(
        flat(g[:, :, -2:], s[:, :, -1:]), flat(g[:, :, :2], s[:, :, :1]), Z
    )
    n = g.shape[0] * g.shape[1] * 2

    def faces(rows):
        return (
            rows[:n].reshape(g.shape[:2] + (2, C)),
            rows[n:].reshape(s.shape[:2] + (1, C)),
        )

    (g_lo, s_lo), (g_hi, s_hi) = faces(up), faces(down)
    rest = PITCH - nz - 4
    g = jnp.concatenate(
        [g_lo, g, g_hi, jnp.zeros(g.shape[:2] + (rest, C), BF16)], axis=2
    )
    edge = jnp.zeros(s.shape[:2] + (1, C), BF16)
    edge_end = jnp.zeros(s.shape[:2] + (rest + 1, C), BF16)
    s = jnp.concatenate([edge, s_lo, s, s_hi, edge_end], axis=2)
    return g, s


def pitched(cells):
    nx, ny, nz, _ = cells.shape
    return jnp.pad(cells, ((0, 0), (0, 0), (2, PITCH - nz - 2), (0, 0)))


def shifted_into(out_ref, cells):
    lead = cells.shape[:-1]
    rows = cells.reshape(-1, C)
    n = rows.shape[0]
    out_ref[..., :C] = pltpu.roll(rows, n - 1, 0).astype(BF16).reshape(lead + (C,))
    out_ref[..., C : 2 * C] = cells.astype(BF16)
    out_ref[..., 2 * C :] = pltpu.roll(rows, 1, 0).astype(BF16).reshape(lead + (C,))


def taps():
    return [(a, b) for a in range(3) for b in range(3)]


def window(ref, start_x, start_y, nx, ny):
    return ref[start_x : start_x + nx, start_y : start_y + ny].reshape(
        nx * ny * PITCH, 3 * C
    )


def kernel_grads(act_t, ref, first_x, first_y, nx, ny, scale, out_ref, slot):
    for t, (a, b) in enumerate(taps()):
        part = jnp.dot(
            act_t,
            window(ref, first_x - a, first_y - b, nx, ny),
            preferred_element_type=F32,
        )
        part = (part * scale).astype(BF16)
        for k in range(3):
            out_ref[slot, t * 3 + k] = part[:, k * C : (k + 1) * C]


def input_grads(ref, w_ref, first_x, first_y, nx, ny):
    total = None
    for t, (a, b) in enumerate(taps()):
        part = jnp.dot(
            window(ref, first_x - a, first_y - b, nx, ny),
            w_ref[t],
            preferred_element_type=F32,
        )
        total = part if total is None else total + part
    return total


def main_kernel(
    scale, core_ref, g_ref, s_ref, hidden_ref, input_ref, w_ref, grads_ref, g_one_ref, wide_two, wide_one
):
    core = core_ref[0]
    nx, ny = hidden_ref.shape[:2]
    shifted_into(wide_two, g_ref[...].astype(F32))
    hidden_t = hidden_ref[...].reshape(-1, C).T
    kernel_grads(hidden_t, wide_two, 3, 3, nx, ny, scale, grads_ref, 1 - core)
    d_hidden = input_grads(wide_two, w_ref, 2, 2, nx + 2, ny + 2)
    side = s_ref[...].astype(F32).reshape(-1, C)
    slope = jnp.where(side > 0, 1.0, jnp.where(side < 0, slope_low, 0.0))
    g_one = (d_hidden * slope).astype(BF16).reshape(s_ref.shape)
    shifted_into(wide_one, g_one.astype(F32))
    g_one_ref[...] = wide_one[...]
    input_t = input_ref[...].reshape(-1, C).T
    kernel_grads(input_t, wide_one, 2, 2, nx, ny, scale, grads_ref, core)


def input_kernel(wide_ref, w_ref, out_ref):
    nx, ny, nz, _ = out_ref.shape
    total = input_grads(wide_ref, w_ref, 2, 2, nx, ny)
    out_ref[...] = total.reshape(nx, ny, PITCH, C)[:, :, 2 : 2 + nz].astype(BF16)


def vmem():
    return pl.BlockSpec(memory_space=pltpu.VMEM)


def wide_weight(weight):
    return weight.transpose(0, 1, 2, 4, 3).reshape(9, 3 * C, C)


def reduced(grads):
    got = lax.ppermute(grads[1], "gc", [(0, 1), (1, 0)])
    mine = (grads[0].astype(F32) + got.astype(F32)).astype(BF16)
    groups = lax.axis_size(REDUCE)
    rows = mine.reshape(-1, PITCH, C)
    used = rows.shape[0]
    rows = jnp.pad(rows, ((0, groups - used), (0, 0), (0, 0)))
    parts = lax.all_to_all(rows, REDUCE, 0, 0, tiled=True)
    total = jnp.sum(parts.astype(F32), axis=0).astype(BF16)
    spread = jnp.broadcast_to(total[None], (groups,) + total.shape)
    spread = lax.all_to_all(spread, REDUCE, 0, 0, tiled=True)
    return spread[:used].reshape(grads.shape[1:])


def on_device(cells_all, layer_input, pre_one, pre_two, out_grad, weight_one, weight_two):
    nx, ny, nz, _ = layer_input.shape
    core = lax.axis_index("gc")
    pre_one_f = pre_one.astype(F32)
    hidden = (pre_one_f * jnp.where(pre_one_f > 0, 1.0, slope_low)).astype(BF16)
    side = jnp.where(pre_one_f > 0, 1.0, -1.0).astype(BF16)
    slope_two = jnp.where(pre_two.astype(F32) > 0, 1.0, slope_low)
    g_two = (out_grad.astype(F32) * slope_two).astype(BF16)
    g_two, side = extend(g_two, side)

    taps_flops = 2 * 27 * C * C
    cells = nx * ny * PITCH
    grads, wide_one = pl.pallas_call(
        functools.partial(main_kernel, float(cells_all) ** -0.5),
        out_shape=(
            jax.ShapeDtypeStruct((2, 27, C, C), BF16),
            jax.ShapeDtypeStruct((nx + 2, ny + 2, PITCH, 3 * C), BF16),
        ),
        in_specs=[pl.BlockSpec(memory_space=pltpu.SMEM)] + [vmem()] * 5,
        out_specs=(vmem(), vmem()),
        scratch_shapes=[
            pltpu.VMEM((nx + 4, ny + 4, PITCH, 3 * C), BF16),
            pltpu.VMEM((nx + 2, ny + 2, PITCH, 3 * C), BF16),
        ],
        compiler_params=pltpu.CompilerParams(vmem_limit_bytes=40 * 2**20),
        cost_estimate=pl.CostEstimate(
            flops=4 * cells * taps_flops, bytes_accessed=6 * 2**20, transcendentals=0
        ),
        name="kernel_gradients",
    )(
        core.reshape(1).astype(jnp.int32),
        g_two,
        side,
        pitched(hidden),
        pitched(layer_input),
        wide_weight(weight_two),
    )
    input_grad = pl.pallas_call(
        input_kernel,
        out_shape=jax.ShapeDtypeStruct((nx, ny, nz, C), BF16),
        in_specs=[vmem()] * 2,
        out_specs=vmem(),
        compiler_params=pltpu.CompilerParams(vmem_limit_bytes=40 * 2**20),
        cost_estimate=pl.CostEstimate(
            flops=cells * taps_flops, bytes_accessed=2 * 2**20, transcendentals=0
        ),
        name="input_gradient",
    )(wide_one, wide_weight(weight_one))

    mine = reduced(grads)
    other = lax.ppermute(mine, "gc", [(0, 1), (1, 0)])
    first = core == 0
    shape = weight_one.shape
    grad_one = jnp.where(first, mine, other).reshape(shape)
    grad_two = jnp.where(first, other, mine).reshape(shape)
    return input_grad, grad_one, grad_two


def solution(mesh):
    sizes = mesh.devices.shape
    cores, rows = 2, sizes[2] // 4
    devices = mesh.devices.reshape(sizes[0], sizes[1], 2, rows, cores)
    fine = Mesh(devices, ("gx", "gy", "gh", "gw", "gc"))
    split = P("gx", "gy", Z, None)

    def whole(*arrays):
        cells_all = 1
        for size in arrays[0].shape[:3]:
            cells_all *= size
        return jax.shard_map(
            functools.partial(on_device, cells_all),
            mesh=fine,
            in_specs=(split, split, split, split, P(), P()),
            out_specs=(split, P(), P()),
            check_vma=False,
        )(*arrays)

    return whole
```

```python
import functools

import jax
import jax.numpy as jnp
from jax import lax
from jax.experimental import pallas as pl
from jax.experimental.pallas import tpu as pltpu
from jax.sharding import Mesh
from jax.sharding import PartitionSpec as P

slope_low = 0.3
Z = ("gh", "gw", "gc")
NEAR = ("gx", "gw")
FAR = ("gy", "gh")
C = 128
PITCH = 16
F32 = jnp.float32
BF16 = jnp.bfloat16


def exchange(up, down, axis):
    peers = lax.axis_size(axis)
    right = [(i, i + 1) for i in range(peers - 1)]
    left = [(i + 1, i) for i in range(peers - 1)]
    return lax.ppermute(up, axis, right), lax.ppermute(down, axis, left)


def pack(g, s):
    lines = g.shape[2]
    return jnp.concatenate(
        [g.reshape(-1, lines, C), s.reshape(-1, lines, C)], axis=0
    )


def unpack(rows, g_shape, s_shape):
    n = g_shape[0] * g_shape[1]
    return rows[:n].reshape(g_shape), rows[n:].reshape(s_shape)


def extend(g, s):
    nx, ny, nz, _ = g.shape
    up, down = exchange(pack(g[-2:], s[-1:]), pack(g[:2], s[:1]), "gx")
    shapes = ((2, ny, nz, C), (1, ny, nz, C))
    (g_lo, s_lo), (g_hi, s_hi) = unpack(up, *shapes), unpack(down, *shapes)
    g = jnp.concatenate([g_lo, g, g_hi], axis=0)
    s = jnp.concatenate([s_lo, s, s_hi], axis=0)

    up, down = exchange(
        pack(g[:, -2:], s[:, -1:]), pack(g[:, :2], s[:, :1]), "gy"
    )
    shapes = ((nx + 4, 2, nz, C), (nx + 2, 1, nz, C))
    (g_lo, s_lo), (g_hi, s_hi) = unpack(up, *shapes), unpack(down, *shapes)
    g = jnp.concatenate([g_lo, g, g_hi], axis=1)
    s = jnp.concatenate([s_lo, s, s_hi], axis=1)

    def flat(g_face, s_face):
        return jnp.concatenate(
            [g_face.reshape(-1, C), s_face.reshape(-1, C)], axis=0
        )

    up, down = exchange(
        flat(g[:, :, -2:], s[:, :, -1:]), flat(g[:, :, :2], s[:, :, :1]), Z
    )
    n = g.shape[0] * g.shape[1] * 2

    def faces(rows):
        return (
            rows[:n].reshape(g.shape[:2] + (2, C)),
            rows[n:].reshape(s.shape[:2] + (1, C)),
        )

    (g_lo, s_lo), (g_hi, s_hi) = faces(up), faces(down)
    rest = PITCH - nz - 4
    g = jnp.concatenate(
        [g_lo, g, g_hi, jnp.zeros(g.shape[:2] + (rest, C), BF16)], axis=2
    )
    edge = jnp.zeros(s.shape[:2] + (1, C), BF16)
    edge_end = jnp.zeros(s.shape[:2] + (rest + 1, C), BF16)
    s = jnp.concatenate([edge, s_lo, s, s_hi, edge_end], axis=2)
    return g, s


def pitched(cells):
    nx, ny, nz, _ = cells.shape
    return jnp.pad(cells, ((0, 0), (0, 0), (2, PITCH - nz - 2), (0, 0)))


def shifted_into(out_ref, cells):
    lead = cells.shape[:-1]
    rows = cells.reshape(-1, C)
    n = rows.shape[0]
    out_ref[..., :C] = pltpu.roll(rows, n - 1, 0).astype(BF16).reshape(lead + (C,))
    out_ref[..., C : 2 * C] = cells.astype(BF16)
    out_ref[..., 2 * C :] = pltpu.roll(rows, 1, 0).astype(BF16).reshape(lead + (C,))


def taps():
    return [(a, b) for a in range(3) for b in range(3)]


def window(ref, start_x, start_y, nx, ny):
    return ref[start_x : start_x + nx, start_y : start_y + ny].reshape(
        nx * ny * PITCH, 3 * C
    )


def kernel_grads(act_t, ref, first_x, first_y, nx, ny, scale, out_ref, slot):
    for t, (a, b) in enumerate(taps()):
        part = jnp.dot(
            act_t,
            window(ref, first_x - a, first_y - b, nx, ny),
            preferred_element_type=F32,
        )
        part = (part * scale).astype(BF16)
        for k in range(3):
            out_ref[slot, t * 3 + k] = part[:, k * C : (k + 1) * C]


def input_grads(ref, w_ref, first_x, first_y, nx, ny):
    total = None
    for t, (a, b) in enumerate(taps()):
        part = jnp.dot(
            window(ref, first_x - a, first_y - b, nx, ny),
            w_ref[t],
            preferred_element_type=F32,
        )
        total = part if total is None else total + part
    return total


def main_kernel(
    scale, core_ref, g_ref, s_ref, hidden_ref, input_ref, w_ref, grads_ref, g_one_ref, wide_two, wide_one
):
    core = core_ref[0]
    grads_ref[:, 27] = jnp.zeros((2, C, C), BF16)
    nx, ny = hidden_ref.shape[:2]
    shifted_into(wide_two, g_ref[...].astype(F32))
    hidden_t = hidden_ref[...].reshape(-1, C).T
    kernel_grads(hidden_t, wide_two, 3, 3, nx, ny, scale, grads_ref, 1 - core)
    d_hidden = input_grads(wide_two, w_ref, 2, 2, nx + 2, ny + 2)
    side = s_ref[...].astype(F32).reshape(-1, C)
    slope = jnp.where(side > 0, 1.0, jnp.where(side < 0, slope_low, 0.0))
    g_one = (d_hidden * slope).astype(BF16).reshape(s_ref.shape)
    shifted_into(wide_one, g_one.astype(F32))
    g_one_ref[...] = wide_one[...]
    input_t = input_ref[...].reshape(-1, C).T
    kernel_grads(input_t, wide_one, 2, 2, nx, ny, scale, grads_ref, core)


def input_kernel(wide_ref, w_ref, out_ref):
    nx, ny, nz, _ = out_ref.shape
    total = input_grads(wide_ref, w_ref, 2, 2, nx, ny)
    out_ref[...] = total.reshape(nx, ny, PITCH, C)[:, :, 2 : 2 + nz].astype(BF16)


def vmem():
    return pl.BlockSpec(memory_space=pltpu.VMEM)


def wide_weight(weight):
    return weight.transpose(0, 1, 2, 4, 3).reshape(9, 3 * C, C)


def spread(rows, axes):
    peers = lax.axis_size(axes)
    copies = jnp.broadcast_to(rows[None], (peers,) + rows.shape)
    return lax.all_to_all(copies, axes, 0, 0, tiled=True)


def added(parts):
    return jnp.sum(parts.astype(F32), axis=0).astype(BF16)


def reduced(grads):
    got = lax.ppermute(grads[1], "gc", [(0, 1), (1, 0)])
    mine = (grads[0].astype(F32) + got.astype(F32)).astype(BF16)
    rows = mine.reshape(lax.axis_size(NEAR), -1, C)
    share = added(lax.all_to_all(rows, NEAR, 0, 0, tiled=True))
    total = added(spread(share, FAR))
    return spread(total, NEAR).reshape(grads.shape[1:])


def on_device(cells_all, layer_input, pre_one, pre_two, out_grad, weight_one, weight_two):
    nx, ny, nz, _ = layer_input.shape
    core = lax.axis_index("gc")
    pre_one_f = pre_one.astype(F32)
    hidden = (pre_one_f * jnp.where(pre_one_f > 0, 1.0, slope_low)).astype(BF16)
    side = jnp.where(pre_one_f > 0, 1.0, -1.0).astype(BF16)
    slope_two = jnp.where(pre_two.astype(F32) > 0, 1.0, slope_low)
    g_two = (out_grad.astype(F32) * slope_two).astype(BF16)
    g_two, side = extend(g_two, side)

    taps_flops = 2 * 27 * C * C
    cells = nx * ny * PITCH
    grads, wide_one = pl.pallas_call(
        functools.partial(main_kernel, float(cells_all) ** -0.5),
        out_shape=(
            jax.ShapeDtypeStruct((2, 28, C, C), BF16),
            jax.ShapeDtypeStruct((nx + 2, ny + 2, PITCH, 3 * C), BF16),
        ),
        in_specs=[pl.BlockSpec(memory_space=pltpu.SMEM)] + [vmem()] * 5,
        out_specs=(vmem(), vmem()),
        scratch_shapes=[
            pltpu.VMEM((nx + 4, ny + 4, PITCH, 3 * C), BF16),
            pltpu.VMEM((nx + 2, ny + 2, PITCH, 3 * C), BF16),
        ],
        compiler_params=pltpu.CompilerParams(vmem_limit_bytes=40 * 2**20),
        cost_estimate=pl.CostEstimate(
            flops=4 * cells * taps_flops, bytes_accessed=6 * 2**20, transcendentals=0
        ),
        name="kernel_gradients",
    )(
        core.reshape(1).astype(jnp.int32),
        g_two,
        side,
        pitched(hidden),
        pitched(layer_input),
        wide_weight(weight_two),
    )
    input_grad = pl.pallas_call(
        input_kernel,
        out_shape=jax.ShapeDtypeStruct((nx, ny, nz, C), BF16),
        in_specs=[vmem()] * 2,
        out_specs=vmem(),
        compiler_params=pltpu.CompilerParams(vmem_limit_bytes=40 * 2**20),
        cost_estimate=pl.CostEstimate(
            flops=cells * taps_flops, bytes_accessed=2 * 2**20, transcendentals=0
        ),
        name="input_gradient",
    )(wide_one, wide_weight(weight_one))

    mine = reduced(grads)
    other = lax.ppermute(mine, "gc", [(0, 1), (1, 0)])
    first = core == 0
    mine, other = mine[:27], other[:27]
    shape = weight_one.shape
    grad_one = jnp.where(first, mine, other).reshape(shape)
    grad_two = jnp.where(first, other, mine).reshape(shape)
    return input_grad, grad_one, grad_two


def solution(mesh):
    sizes = mesh.devices.shape
    cores, rows = 2, sizes[2] // 4
    devices = mesh.devices.reshape(sizes[0], sizes[1], 2, rows, cores)
    fine = Mesh(devices, ("gx", "gy", "gh", "gw", "gc"))
    split = P("gx", "gy", Z, None)

    def whole(*arrays):
        cells_all = 1
        for size in arrays[0].shape[:3]:
            cells_all *= size
        return jax.shard_map(
            functools.partial(on_device, cells_all),
            mesh=fine,
            in_specs=(split, split, split, split, P(), P()),
            out_specs=(split, P(), P()),
            check_vma=False,
        )(*arrays)

    return whole
```

```python
import functools

import jax
import jax.numpy as jnp
from jax import lax
from jax.experimental import pallas as pl
from jax.experimental.pallas import tpu as pltpu
from jax.sharding import Mesh
from jax.sharding import PartitionSpec as P

slope_low = 0.3
Z = ("gh", "gw", "gc")
FAR = ("gy", "gh")
C = 128
PITCH = 16
F32 = jnp.float32
BF16 = jnp.bfloat16


def exchange(up, down, axis):
    peers = lax.axis_size(axis)
    right = [(i, i + 1) for i in range(peers - 1)]
    left = [(i + 1, i) for i in range(peers - 1)]
    return lax.ppermute(up, axis, right), lax.ppermute(down, axis, left)


def pack(g, s):
    lines = g.shape[2]
    return jnp.concatenate(
        [g.reshape(-1, lines, C), s.reshape(-1, lines, C)], axis=0
    )


def unpack(rows, g_shape, s_shape):
    n = g_shape[0] * g_shape[1]
    return rows[:n].reshape(g_shape), rows[n:].reshape(s_shape)


def extend(g, s, upper):
    nx, ny, nz, _ = g.shape
    up, down = exchange(pack(g[-2:], s[-1:]), pack(g[:2], s[:1]), "gx")
    shapes = ((2, ny, nz, C), (1, ny, nz, C))
    (g_lo, s_lo), (g_hi, s_hi) = unpack(up, *shapes), unpack(down, *shapes)
    g = jnp.concatenate([g_lo, g, g_hi], axis=0)
    s = jnp.concatenate([s_lo, s, s_hi], axis=0)

    up, down = exchange(
        pack(g[:, -2:], s[:, -1:]), pack(g[:, :2], s[:, :1]), "gy"
    )
    shapes = ((nx + 4, 2, nz, C), (nx + 2, 1, nz, C))
    (g_lo, s_lo), (g_hi, s_hi) = unpack(up, *shapes), unpack(down, *shapes)
    g = jnp.concatenate([g_lo, g, g_hi], axis=1)
    s = jnp.concatenate([s_lo, s, s_hi], axis=1)

    lines = pack(g, s)
    last, first = lines[:, -2:], lines[:, :2]
    outer, inner = [], []
    for i in range(1, lax.axis_size(Z) - 1, 2):
        outer += [(i, i + 1), (i + 1, i)]
    for i in range(0, lax.axis_size(Z), 2):
        inner += [(i, i + 1), (i + 1, i)]
    far = lax.ppermute(jnp.where(upper, last, first), Z, outer)
    near = lax.ppermute(jnp.where(upper, first, last), Z, inner)
    lo, hi = jnp.where(upper, near, far), jnp.where(upper, far, near)
    rest = jnp.zeros((lines.shape[0], PITCH - nz - 4, C), BF16)
    return jnp.concatenate([lo, lines, hi, rest], axis=1)


def pitched(cells):
    nx, ny, nz, _ = cells.shape
    return jnp.pad(cells, ((0, 0), (0, 0), (2, PITCH - nz - 2), (0, 0)))


def shifted_into(out_ref, cells):
    lead = cells.shape[:-1]
    rows = cells.reshape(-1, C)
    n = rows.shape[0]
    out_ref[..., :C] = pltpu.roll(rows, n - 1, 0).astype(BF16).reshape(lead + (C,))
    out_ref[..., C : 2 * C] = cells.astype(BF16)
    out_ref[..., 2 * C :] = pltpu.roll(rows, 1, 0).astype(BF16).reshape(lead + (C,))


def taps():
    return [(a, b) for a in range(3) for b in range(3)]


def window(ref, start_x, start_y, nx, ny):
    return ref[start_x : start_x + nx, start_y : start_y + ny].reshape(
        nx * ny * PITCH, 3 * C
    )


def kernel_grads(act_t, ref, first_x, first_y, nx, ny, scale, out_ref, slot):
    for t, (a, b) in enumerate(taps()):
        part = jnp.dot(
            act_t,
            window(ref, first_x - a, first_y - b, nx, ny),
            preferred_element_type=F32,
        )
        part = (part * scale).astype(BF16)
        for k in range(3):
            out_ref[slot, t * 3 + k] = part[:, k * C : (k + 1) * C]


def input_grads(ref, w_ref, first_x, first_y, nx, ny):
    total = None
    for t, (a, b) in enumerate(taps()):
        weight = jnp.concatenate([w_ref[3 * t + k] for k in range(3)], axis=1)
        part = lax.dot_general(
            window(ref, first_x - a, first_y - b, nx, ny),
            weight,
            (((1,), (1,)), ((), ())),
            preferred_element_type=F32,
        )
        total = part if total is None else total + part
    return total


def main_kernel(
    scale, core_ref, lines_ref, hidden_ref, input_ref, w_ref, grads_ref, g_one_ref, wide_two, wide_one
):
    core = core_ref[0]
    grads_ref[:, 27] = jnp.zeros((2, C, C), BF16)
    nx, ny = hidden_ref.shape[:2]
    split = (nx + 4) * (ny + 4)
    shifted_into(wide_two, lines_ref[:split].astype(F32).reshape(nx + 4, ny + 4, PITCH, C))
    hidden_t = hidden_ref[...].reshape(-1, C).T
    kernel_grads(hidden_t, wide_two, 3, 3, nx, ny, scale, grads_ref, 1 - core)
    d_hidden = input_grads(wide_two, w_ref, 2, 2, nx + 2, ny + 2)
    side = lines_ref[split:].astype(F32).reshape(-1, C)
    slope = jnp.where(side > 0, 1.0, jnp.where(side < 0, slope_low, 0.0))
    g_one = (d_hidden * slope).astype(BF16).reshape(nx + 2, ny + 2, PITCH, C)
    shifted_into(wide_one, g_one.astype(F32))
    g_one_ref[...] = wide_one[...]
    input_t = input_ref[...].reshape(-1, C).T
    kernel_grads(input_t, wide_one, 2, 2, nx, ny, scale, grads_ref, core)


def input_kernel(wide_ref, w_ref, out_ref):
    nx, ny, nz, _ = out_ref.shape
    total = input_grads(wide_ref, w_ref, 2, 2, nx, ny)
    out_ref[...] = total.reshape(nx, ny, PITCH, C)[:, :, 2 : 2 + nz].astype(BF16)


def vmem():
    return pl.BlockSpec(memory_space=pltpu.VMEM)


def place_kernel(core_ref, mine_ref, other_ref, one_ref, two_ref, sems):
    n = one_ref.shape[0]
    parts = sems.shape[1]
    step = n // parts
    for core, (one, two) in enumerate(((mine_ref, other_ref), (other_ref, mine_ref))):

        @pl.when(core_ref[0] == core)
        def _():
            copies = []
            for part in range(parts):
                rows = pl.ds(part * step, step)
                for i, (source, result) in enumerate(((one, one_ref), (two, two_ref))):
                    copies.append(
                        pltpu.make_async_copy(
                            source.at[rows], result.at[rows], sems.at[i, part]
                        )
                    )
            for copy in copies:
                copy.start()
            for copy in copies:
                copy.wait()


def spread(rows, axes):
    peers = lax.axis_size(axes)
    copies = jnp.broadcast_to(rows[None], (peers,) + rows.shape)
    return lax.all_to_all(copies, axes, 0, 0, tiled=True)


def scattered(rows, axis):
    pieces = rows.reshape(lax.axis_size(axis), -1, C)
    return lax.all_to_all(pieces, axis, 0, 0, tiled=True)


def added(parts):
    return jnp.sum(parts.astype(F32), axis=0).astype(BF16)


def reduced(grads):
    got = lax.ppermute(grads[1], "gc", [(0, 1), (1, 0)])
    mine = (grads[0].astype(F32) + got.astype(F32)).astype(BF16)
    share = added(scattered(mine.reshape(-1, C), "gx"))
    share = added(scattered(share, "gw"))
    total = added(spread(share, FAR))
    total = spread(total, "gw").reshape(-1, C)
    return spread(total, "gx").reshape(grads.shape[1:])


def on_device(cells_all, layer_input, pre_one, pre_two, out_grad, weight_one, weight_two):
    nx, ny, nz, _ = layer_input.shape
    core = lax.axis_index("gc").reshape(1).astype(jnp.int32)
    pre_one_f = pre_one.astype(F32)
    hidden = (pre_one_f * jnp.where(pre_one_f > 0, 1.0, slope_low)).astype(BF16)
    side = jnp.where(pre_one_f > 0, 1.0, -1.0).astype(BF16)
    slope_two = jnp.where(pre_two.astype(F32) > 0, 1.0, slope_low)
    g_two = (out_grad.astype(F32) * slope_two).astype(BF16)
    lines = extend(g_two, side, core[0] == 1)

    taps_flops = 2 * 27 * C * C
    cells = nx * ny * PITCH
    grads, wide_one = pl.pallas_call(
        functools.partial(main_kernel, float(cells_all) ** -0.5),
        out_shape=(
            jax.ShapeDtypeStruct((2, 28, C, C), BF16),
            jax.ShapeDtypeStruct((nx + 2, ny + 2, PITCH, 3 * C), BF16),
        ),
        in_specs=[pl.BlockSpec(memory_space=pltpu.SMEM)] + [vmem()] * 4,
        out_specs=(vmem(), vmem()),
        scratch_shapes=[
            pltpu.VMEM((nx + 4, ny + 4, PITCH, 3 * C), BF16),
            pltpu.VMEM((nx + 2, ny + 2, PITCH, 3 * C), BF16),
        ],
        compiler_params=pltpu.CompilerParams(vmem_limit_bytes=16 * 2**20),
        cost_estimate=pl.CostEstimate(
            flops=4 * cells * taps_flops, bytes_accessed=6 * 2**20, transcendentals=0
        ),
        name="kernel_gradients",
    )(
        core,
        lines,
        pitched(hidden),
        pitched(layer_input),
        weight_two.reshape(27, C, C),
    )
    input_grad = pl.pallas_call(
        input_kernel,
        out_shape=jax.ShapeDtypeStruct((nx, ny, nz, C), BF16),
        in_specs=[vmem()] * 2,
        out_specs=vmem(),
        compiler_params=pltpu.CompilerParams(vmem_limit_bytes=8 * 2**20),
        cost_estimate=pl.CostEstimate(
            flops=cells * taps_flops, bytes_accessed=2 * 2**20, transcendentals=0
        ),
        name="input_gradient",
    )(wide_one, weight_one.reshape(27, C, C))

    mine = reduced(grads)
    other = lax.ppermute(mine, "gc", [(0, 1), (1, 0)])
    total_type = jax.ShapeDtypeStruct((27, C, C), BF16)
    grad_one, grad_two = pl.pallas_call(
        place_kernel,
        out_shape=(total_type, total_type),
        in_specs=[pl.BlockSpec(memory_space=pltpu.SMEM)]
        + [pl.BlockSpec(memory_space=pl.ANY)] * 2,
        out_specs=(pl.BlockSpec(memory_space=pl.ANY),) * 2,
        scratch_shapes=[pltpu.SemaphoreType.DMA((2, 9))],
        compiler_params=pltpu.CompilerParams(vmem_limit_bytes=2**20),
        name="place_totals",
    )(core, mine, other)
    shape = weight_one.shape
    return input_grad, grad_one.reshape(shape), grad_two.reshape(shape)


def solution(mesh):
    sizes = mesh.devices.shape
    cores, rows = 2, sizes[2] // 4
    devices = mesh.devices.reshape(sizes[0], sizes[1], 2, rows, cores)
    fine = Mesh(devices, ("gx", "gy", "gh", "gw", "gc"))
    split = P("gx", "gy", Z, None)

    def whole(*arrays):
        cells_all = 1
        for size in arrays[0].shape[:3]:
            cells_all *= size
        return jax.shard_map(
            functools.partial(on_device, cells_all),
            mesh=fine,
            in_specs=(split, split, split, split, P(), P()),
            out_specs=(split, P(), P()),
            check_vma=False,
        )(*arrays)

    return whole
```

```python
import functools

import jax
import jax.numpy as jnp
from jax import lax
from jax.experimental import pallas as pl
from jax.experimental.pallas import tpu as pltpu
from jax.sharding import Mesh
from jax.sharding import PartitionSpec as P

slope_low = 0.3
Z = ("gh", "gw", "gc")
RING = ("gy", "gh")
C = 128
GROUP = 2
PITCH = 16
F32 = jnp.float32
BF16 = jnp.bfloat16


def exchange(up, down, axis):
    peers = lax.axis_size(axis)
    right = [(i, i + 1) for i in range(peers - 1)]
    left = [(i + 1, i) for i in range(peers - 1)]
    return lax.ppermute(up, axis, right), lax.ppermute(down, axis, left)


def pack(g, s):
    lines = g.shape[2]
    return jnp.concatenate(
        [g.reshape(-1, lines, C), s.reshape(-1, lines, C)], axis=0
    )


def unpack(rows, g_shape, s_shape):
    n = g_shape[0] * g_shape[1]
    return rows[:n].reshape(g_shape), rows[n:].reshape(s_shape)


def extend(g, s, upper):
    nx, ny, nz, _ = g.shape
    up, down = exchange(pack(g[-2:], s[-1:]), pack(g[:2], s[:1]), "gx")
    shapes = ((2, ny, nz, C), (1, ny, nz, C))
    (g_lo, s_lo), (g_hi, s_hi) = unpack(up, *shapes), unpack(down, *shapes)
    g = jnp.concatenate([g_lo, g, g_hi], axis=0)
    s = jnp.concatenate([s_lo, s, s_hi], axis=0)

    up, down = exchange(
        pack(g[:, -2:], s[:, -1:]), pack(g[:, :2], s[:, :1]), "gy"
    )
    shapes = ((nx + 4, 2, nz, C), (nx + 2, 1, nz, C))
    (g_lo, s_lo), (g_hi, s_hi) = unpack(up, *shapes), unpack(down, *shapes)
    g = jnp.concatenate([g_lo, g, g_hi], axis=1)
    s = jnp.concatenate([s_lo, s, s_hi], axis=1)

    lines = pack(g, s)
    last, first = lines[:, -2:], lines[:, :2]
    outer, inner = [], []
    for i in range(1, lax.axis_size(Z) - 1, 2):
        outer += [(i, i + 1), (i + 1, i)]
    for i in range(0, lax.axis_size(Z), 2):
        inner += [(i, i + 1), (i + 1, i)]
    far = lax.ppermute(jnp.where(upper, last, first), Z, outer)
    near = lax.ppermute(jnp.where(upper, first, last), Z, inner)
    lo, hi = jnp.where(upper, near, far), jnp.where(upper, far, near)
    rest = jnp.zeros((lines.shape[0], PITCH - nz - 4, C), BF16)
    return jnp.concatenate([lo, lines, hi, rest], axis=1)


def paired(cells):
    half = cells.shape[1] // 2
    return jnp.concatenate([cells[:, :half], cells[:, half:]], axis=2)


def moved(rows, by):
    n = rows.shape[0]
    return rows if by == 0 else pltpu.roll(rows, (n - by) % n, 0)


def wide_into(out_ref, cells):
    rows = cells.reshape(-1, C)
    for k in range(3):
        out_ref[..., k * C : (k + 1) * C] = (
            moved(rows, 1 - k).astype(BF16).reshape(cells.shape)
        )


def pairs_into(out_ref, cells, first):
    nx, ny = cells.shape[:2]
    rows = cells.reshape(-1, C)
    held = out_ref.shape[1]
    half = held - 2
    for k in range(3):
        lines = moved(rows, 3 - k).reshape(nx, ny, PITCH, C)[:, :, : PITCH // 2]
        low = lines[:, first : first + held]
        high = lines[:, first + half : first + half + held]
        out_ref[..., k * C : (k + 1) * C] = jnp.concatenate(
            [low, high], axis=2
        ).astype(BF16)


def taps():
    return [(a, b) for a in range(3) for b in range(3)]


def window(ref, tap, nx, ny):
    a, b = tap
    return ref[2 - a : 2 - a + nx, 2 - b : 2 - b + ny].reshape(nx * ny * PITCH, 3 * C)


def kernel_grads(act_t, ref, scale, out_ref, slot):
    nx, half = ref.shape[0] - 2, ref.shape[1] - 2
    for t, tap in enumerate(taps()):
        part = jnp.dot(
            act_t, window(ref, tap, nx, half), preferred_element_type=F32
        )
        part = (part * scale).astype(BF16)
        for k in range(3):
            out_ref[slot, t * 3 + k] = part[:, k * C : (k + 1) * C]


def input_grads(ref, w_ref, nx, ny):
    total = None
    for group in range(0, 9, GROUP):
        numbers = range(group, min(group + GROUP, 9))
        cells = [window(ref, taps()[t], nx, ny) for t in numbers]
        weights = [w_ref[3 * t + k] for t in numbers for k in range(3)]
        part = lax.dot_general(
            jnp.concatenate(cells, axis=1),
            jnp.concatenate(weights, axis=1),
            (((1,), (1,)), ((), ())),
            preferred_element_type=F32,
        )
        total = part if total is None else total + part
    return total


def main_kernel(
    scale, core_ref, lines_ref, hidden_ref, input_ref, w_ref, grads_ref, pair_one, wide, pair_two
):
    core = core_ref[0]
    nx, half = hidden_ref.shape[:2]
    ny = 2 * half
    split = (nx + 4) * (ny + 4)
    lines = lines_ref[:split].astype(F32).reshape(nx + 4, ny + 4, PITCH, C)
    wide_into(wide, lines)
    pairs_into(pair_two, lines[1 : nx + 3], 1)
    d_hidden = input_grads(wide, w_ref, nx + 2, ny + 2)
    side = lines_ref[split:].astype(F32).reshape(-1, C)
    slope = jnp.where(side > 0, 1.0, jnp.where(side < 0, slope_low, 0.0))
    g_one = (d_hidden * slope).astype(BF16).astype(F32)
    pairs_into(pair_one, g_one.reshape(nx + 2, ny + 2, PITCH, C), 0)
    hidden_t = hidden_ref[...].reshape(-1, C).T
    kernel_grads(hidden_t, pair_two, scale, grads_ref, 1 - core)
    input_t = input_ref[...].reshape(-1, C).T
    kernel_grads(input_t, pair_one, scale, grads_ref, core)


def input_kernel(core_ref, pair_ref, w_ref, mine_ref, out_ref, one_ref, two_ref, sems):
    def start(target):
        for copy in chunks(mine_ref, target, sems):
            copy.start()

    def finish(target):
        for copy in chunks(mine_ref, target, sems):
            copy.wait()

    on_core(core_ref, one_ref, two_ref, start)
    nx, ny, nz, _ = out_ref.shape
    half = ny // 2
    total = input_grads(pair_ref, w_ref, nx, half)
    total = total.reshape(nx, half, PITCH, C).astype(BF16)
    out_ref[:, :half] = total[:, :, :nz]
    out_ref[:, half:] = total[:, :, nz:]
    on_core(core_ref, one_ref, two_ref, finish)


def vmem():
    return pl.BlockSpec(memory_space=pltpu.VMEM)


def chunks(source, target, sems):
    step = target.shape[0] // sems.shape[0]
    copies = []
    for part in range(sems.shape[0]):
        rows = pl.ds(part * step, step)
        copies.append(
            pltpu.make_async_copy(source.at[rows], target.at[rows], sems.at[part])
        )
    return copies


def on_core(core_ref, first, second, act):
    for core, target in enumerate((first, second)):

        @pl.when(core_ref[0] == core)
        def _():
            act(target)


def place_kernel(core_ref, other_ref, _, __, one_ref, two_ref, sems):
    def run(target):
        copies = chunks(other_ref, target, sems)
        for copy in copies:
            copy.start()
        for copy in copies:
            copy.wait()

    on_core(core_ref, two_ref, one_ref, run)


def spread(rows, axes):
    peers = lax.axis_size(axes)
    copies = jnp.broadcast_to(rows[None], (peers,) + rows.shape)
    return lax.all_to_all(copies, axes, 0, 0, tiled=True)


def scattered(rows, axis):
    pieces = rows.reshape(lax.axis_size(axis), -1, C)
    return lax.all_to_all(pieces, axis, 0, 0, tiled=True)


def added(parts):
    return jnp.sum(parts.astype(F32), axis=0).astype(BF16)


def reduced(grads):
    got = lax.ppermute(grads[1], "gc", [(0, 1), (1, 0)])
    mine = (grads[0].astype(F32) + got.astype(F32)).astype(BF16)
    share = added(scattered(mine.reshape(-1, C), "gx"))
    used = share.shape[0]
    rest = -used % (lax.axis_size(RING) * PITCH)
    share = added(scattered(jnp.pad(share, ((0, rest), (0, 0))), RING))
    total = added(spread(share, "gw"))
    total = spread(total, RING).reshape(-1, C)[:used]
    return spread(total, "gx").reshape(grads.shape[1:])


def on_device(cells_all, layer_input, pre_one, pre_two, out_grad, weight_one, weight_two):
    nx, ny, nz, _ = layer_input.shape
    core = lax.axis_index("gc").reshape(1).astype(jnp.int32)
    pre_one_f = pre_one.astype(F32)
    hidden = (pre_one_f * jnp.where(pre_one_f > 0, 1.0, slope_low)).astype(BF16)
    side = jnp.where(pre_one_f > 0, 1.0, -1.0).astype(BF16)
    slope_two = jnp.where(pre_two.astype(F32) > 0, 1.0, slope_low)
    g_two = (out_grad.astype(F32) * slope_two).astype(BF16)
    both = lax.optimization_barrier(jnp.concatenate([g_two, side], axis=0))
    g_two, side = both[:nx], both[nx:]
    lines = extend(g_two, side, core[0] == 1)

    taps_flops = 2 * 27 * C * C
    cells = nx * ny * nz
    pair_type = (nx + 2, ny // 2 + 2, PITCH, 3 * C)
    grads, pair_one = pl.pallas_call(
        functools.partial(main_kernel, float(cells_all) ** -0.5),
        out_shape=(
            jax.ShapeDtypeStruct((2, 27, C, C), BF16),
            jax.ShapeDtypeStruct(pair_type, BF16),
        ),
        in_specs=[pl.BlockSpec(memory_space=pltpu.SMEM)] + [vmem()] * 4,
        out_specs=(vmem(), vmem()),
        scratch_shapes=[
            pltpu.VMEM((nx + 4, ny + 4, PITCH, 3 * C), BF16),
            pltpu.VMEM(pair_type, BF16),
        ],
        compiler_params=pltpu.CompilerParams(vmem_limit_bytes=16 * 2**20),
        cost_estimate=pl.CostEstimate(
            flops=4 * cells * taps_flops, bytes_accessed=6 * 2**20, transcendentals=0
        ),
        name="kernel_gradients",
    )(
        core,
        lines,
        paired(hidden),
        paired(layer_input),
        weight_two.reshape(27, C, C),
    )
    mine = reduced(grads)
    other = lax.ppermute(mine, "gc", [(0, 1), (1, 0)])
    smem = pl.BlockSpec(memory_space=pltpu.SMEM)
    anywhere = pl.BlockSpec(memory_space=pl.ANY)
    total_type = jax.ShapeDtypeStruct((27, C, C), BF16)
    input_grad, grad_one, grad_two = pl.pallas_call(
        input_kernel,
        out_shape=(
            jax.ShapeDtypeStruct((nx, ny, nz, C), BF16),
            total_type,
            total_type,
        ),
        in_specs=[smem, vmem(), vmem(), anywhere],
        out_specs=(vmem(), anywhere, anywhere),
        scratch_shapes=[pltpu.SemaphoreType.DMA((9,))],
        compiler_params=pltpu.CompilerParams(vmem_limit_bytes=8 * 2**20),
        cost_estimate=pl.CostEstimate(
            flops=cells * taps_flops, bytes_accessed=2 * 2**20, transcendentals=0
        ),
        name="input_gradient",
    )(core, pair_one, weight_one.reshape(27, C, C), mine)
    grad_one, grad_two = pl.pallas_call(
        place_kernel,
        out_shape=(total_type, total_type),
        in_specs=[smem] + [anywhere] * 3,
        out_specs=(anywhere, anywhere),
        scratch_shapes=[pltpu.SemaphoreType.DMA((9,))],
        input_output_aliases={2: 0, 3: 1},
        compiler_params=pltpu.CompilerParams(vmem_limit_bytes=2**20),
        name="place_totals",
    )(core, other, grad_one, grad_two)
    shape = weight_one.shape
    return input_grad, grad_one.reshape(shape), grad_two.reshape(shape)


def solution(mesh):
    sizes = mesh.devices.shape
    cores, rows = 2, sizes[2] // 4
    devices = mesh.devices.reshape(sizes[0], sizes[1], 2, rows, cores)
    fine = Mesh(devices, ("gx", "gy", "gh", "gw", "gc"))
    split = P("gx", "gy", Z, None)

    def whole(*arrays):
        cells_all = 1
        for size in arrays[0].shape[:3]:
            cells_all *= size
        return jax.shard_map(
            functools.partial(on_device, cells_all),
            mesh=fine,
            in_specs=(split, split, split, split, P(), P()),
            out_specs=(split, P(), P()),
            check_vma=False,
        )(*arrays)

    return whole
```

```python
import functools

import jax
import jax.numpy as jnp
from jax import lax
from jax.experimental import pallas as pl
from jax.experimental.pallas import tpu as pltpu
from jax.sharding import Mesh
from jax.sharding import PartitionSpec as P
import numpy as np

slope_low = 0.3
Z = ("gh", "gw", "gc")
EVERY = ("gx", "gy", "gh", "gw", "gc")
C = 128
GROUP = 9
PITCH = 16
F32 = jnp.float32
BF16 = jnp.bfloat16


def exchange(up, down, axis):
    peers = lax.axis_size(axis)
    right = [(i, i + 1) for i in range(peers - 1)]
    left = [(i + 1, i) for i in range(peers - 1)]
    return lax.ppermute(up, axis, right), lax.ppermute(down, axis, left)


def pack(g, s):
    lines = g.shape[2]
    return jnp.concatenate(
        [g.reshape(-1, lines, C), s.reshape(-1, lines, C)], axis=0
    )


def unpack(rows, g_shape, s_shape):
    n = g_shape[0] * g_shape[1]
    return rows[:n].reshape(g_shape), rows[n:].reshape(s_shape)


def extend(g, s, upper):
    nx, ny, nz, _ = g.shape
    up, down = exchange(pack(g[-2:], s[-1:]), pack(g[:2], s[:1]), "gx")
    shapes = ((2, ny, nz, C), (1, ny, nz, C))
    (g_lo, s_lo), (g_hi, s_hi) = unpack(up, *shapes), unpack(down, *shapes)
    g = jnp.concatenate([g_lo, g, g_hi], axis=0)
    s = jnp.concatenate([s_lo, s, s_hi], axis=0)

    up, down = exchange(
        pack(g[:, -2:], s[:, -1:]), pack(g[:, :2], s[:, :1]), "gy"
    )
    shapes = ((nx + 4, 2, nz, C), (nx + 2, 1, nz, C))
    (g_lo, s_lo), (g_hi, s_hi) = unpack(up, *shapes), unpack(down, *shapes)
    g = jnp.concatenate([g_lo, g, g_hi], axis=1)
    s = jnp.concatenate([s_lo, s, s_hi], axis=1)

    lines = pack(g, s)
    last, first = lines[:, -2:], lines[:, :2]
    outer, inner = [], []
    for i in range(1, lax.axis_size(Z) - 1, 2):
        outer += [(i, i + 1), (i + 1, i)]
    for i in range(0, lax.axis_size(Z), 2):
        inner += [(i, i + 1), (i + 1, i)]
    far = lax.ppermute(jnp.where(upper, last, first), Z, outer)
    near = lax.ppermute(jnp.where(upper, first, last), Z, inner)
    lo, hi = jnp.where(upper, near, far), jnp.where(upper, far, near)
    rest = jnp.zeros((lines.shape[0], PITCH - nz - 4, C), BF16)
    return jnp.concatenate([lo, lines, hi, rest], axis=1)


def paired(cells):
    half = cells.shape[1] // 2
    return jnp.concatenate([cells[:, :half], cells[:, half:]], axis=2)


def moved(rows, by):
    n = rows.shape[0]
    return rows if by == 0 else pltpu.roll(rows, (n - by) % n, 0)


def wide_into(out_ref, cells):
    rows = cells.reshape(-1, C)
    for k in range(3):
        out_ref[..., k * C : (k + 1) * C] = (
            moved(rows, 1 - k).astype(BF16).reshape(cells.shape)
        )


def pairs_into(out_ref, cells, first):
    nx, ny = cells.shape[:2]
    rows = cells.reshape(-1, C)
    held = out_ref.shape[1]
    half = held - 2
    for k in range(3):
        lines = moved(rows, 3 - k).reshape(nx, ny, PITCH, C)[:, :, : PITCH // 2]
        low = lines[:, first : first + held]
        high = lines[:, first + half : first + half + held]
        out_ref[..., k * C : (k + 1) * C] = jnp.concatenate(
            [low, high], axis=2
        ).astype(BF16)


def taps():
    return [(a, b) for a in range(3) for b in range(3)]


def window(ref, tap, nx, ny):
    a, b = tap
    return ref[2 - a : 2 - a + nx, 2 - b : 2 - b + ny].reshape(nx * ny * PITCH, 3 * C)


def kernel_grads(act_t, ref, scale, out_ref, slot):
    nx, half = ref.shape[0] - 2, ref.shape[1] - 2
    for t, tap in enumerate(taps()):
        part = jnp.dot(
            act_t, window(ref, tap, nx, half), preferred_element_type=F32
        )
        part = (part * scale).astype(BF16)
        for k in range(3):
            out_ref[slot, t * 3 + k] = part[:, k * C : (k + 1) * C]


def input_grads(ref, w_ref, nx, ny):
    total = None
    for group in range(0, 9, GROUP):
        numbers = range(group, min(group + GROUP, 9))
        cells = [window(ref, taps()[t], nx, ny) for t in numbers]
        weights = [w_ref[3 * t + k] for t in numbers for k in range(3)]
        part = lax.dot_general(
            jnp.concatenate(cells, axis=1),
            jnp.concatenate(weights, axis=1),
            (((1,), (1,)), ((), ())),
            preferred_element_type=F32,
        )
        total = part if total is None else total + part
    return total


def two_planes(ref, w_ref, nx, ny):
    plane = ny * PITCH
    parts = [None] * nx
    rest = None
    for b in range(3):
        weights = [
            jnp.concatenate([w_ref[(a * 3 + b) * 3 + k] for k in range(3)], axis=1)
            for a in range(3)
        ]
        cells = ref[1:, 2 - b : 2 - b + ny].reshape(-1, 3 * C)
        both = lax.dot_general(
            cells,
            jnp.concatenate(weights[:2], axis=0),
            (((1,), (1,)), ((), ())),
            preferred_element_type=F32,
        )
        for x in range(nx):
            for a in range(2):
                first = (x + 1 - a) * plane
                part = both[first : first + plane, a * C : (a + 1) * C]
                parts[x] = part if parts[x] is None else parts[x] + part
        last = lax.dot_general(
            window(ref, (2, b), nx, ny),
            weights[2],
            (((1,), (1,)), ((), ())),
            preferred_element_type=F32,
        )
        rest = last if rest is None else rest + last
    return jnp.concatenate(parts, axis=0) + rest


def main_kernel(
    scale, core_ref, lines_ref, hidden_ref, input_ref, w_ref, grads_ref, pair_one, wide, pair_two
):
    core = core_ref[0]
    nx, half = hidden_ref.shape[:2]
    ny = 2 * half
    split = (nx + 4) * (ny + 4)
    lines = lines_ref[:split].astype(F32).reshape(nx + 4, ny + 4, PITCH, C)
    wide_into(wide, lines)
    pairs_into(pair_two, lines[1 : nx + 3], 1)
    d_hidden = two_planes(wide, w_ref, nx + 2, ny + 2)
    side = lines_ref[split:].astype(F32).reshape(-1, C)
    slope = jnp.where(side > 0, 1.0, jnp.where(side < 0, slope_low, 0.0))
    g_one = (d_hidden * slope).astype(BF16).astype(F32)
    pairs_into(pair_one, g_one.reshape(nx + 2, ny + 2, PITCH, C), 0)
    hidden_t = hidden_ref[...].reshape(-1, C).T
    kernel_grads(hidden_t, pair_two, scale, grads_ref, 1 - core)
    input_t = input_ref[...].reshape(-1, C).T
    kernel_grads(input_t, pair_one, scale, grads_ref, core)


def input_kernel(core_ref, pair_ref, w_ref, mine_ref, out_ref, one_ref, two_ref, sems):
    def start(target):
        for copy in chunks(mine_ref, target, sems):
            copy.start()

    def finish(target):
        for copy in chunks(mine_ref, target, sems):
            copy.wait()

    on_core(core_ref, one_ref, two_ref, start)
    nx, ny, nz, _ = out_ref.shape
    half = ny // 2
    total = input_grads(pair_ref, w_ref, nx, half)
    total = total.reshape(nx, half, PITCH, C).astype(BF16)
    out_ref[:, :half] = total[:, :, :nz]
    out_ref[:, half:] = total[:, :, nz:]
    on_core(core_ref, one_ref, two_ref, finish)


def vmem():
    return pl.BlockSpec(memory_space=pltpu.VMEM)


def chunks(source, target, sems):
    step = target.shape[0] // sems.shape[0]
    copies = []
    for part in range(sems.shape[0]):
        rows = pl.ds(part * step, step)
        copies.append(
            pltpu.make_async_copy(source.at[rows], target.at[rows], sems.at[part])
        )
    return copies


def on_core(core_ref, first, second, act):
    for core, target in enumerate((first, second)):

        @pl.when(core_ref[0] == core)
        def _():
            act(target)


def place_kernel(core_ref, other_ref, _, __, one_ref, two_ref, sems):
    def run(target):
        copies = chunks(other_ref, target, sems)
        for copy in copies:
            copy.start()
        for copy in copies:
            copy.wait()

    on_core(core_ref, two_ref, one_ref, run)


def steps():
    sizes = [lax.axis_size(axis) for axis in EVERY]
    number = np.arange(np.prod(sizes)).reshape(sizes)
    nx, ny, nh, nw, _ = sizes

    def groups(devices, axes):
        size = np.prod([devices.shape[axis] for axis in axes])
        last = range(devices.ndim - len(axes), devices.ndim)
        return np.moveaxis(devices, axes, last).reshape(-1, size)

    zero = number[..., 0]
    one = number[..., 1].reshape(nx, ny // 2, 2, nh, nw // 2, 2)
    near = groups(zero, (0,)), groups(one, (2, 5))
    ring = groups(zero, (1, 2)), groups(one, (0, 1))
    far = groups(zero, (3,)), groups(one, (3, 4))
    return [np.concatenate(both).tolist() for both in (near, ring, far)]


def exchanged(pieces, groups):
    return lax.all_to_all(
        pieces, EVERY, 0, 0, axis_index_groups=groups, tiled=True
    )


def spread(rows, groups):
    return exchanged(
        jnp.broadcast_to(rows[None], (len(groups[0]),) + rows.shape), groups
    )


def scattered(rows, groups):
    return exchanged(rows.reshape(len(groups[0]), -1, C), groups)


def added(parts):
    return jnp.sum(parts.astype(F32), axis=0).astype(BF16)


def reduced(grads):
    got = lax.ppermute(grads[1], "gc", [(0, 1), (1, 0)])
    mine = (grads[0].astype(F32) + got.astype(F32)).astype(BF16)
    near, ring, far = steps()
    share = added(scattered(mine.reshape(-1, C), near))
    used = share.shape[0]
    rest = -used % (len(ring[0]) * PITCH)
    share = added(scattered(jnp.pad(share, ((0, rest), (0, 0))), ring))
    total = added(spread(share, far))
    total = spread(total, ring).reshape(-1, C)[:used]
    return spread(total, near).reshape(grads.shape[1:])


def on_device(cells_all, layer_input, pre_one, pre_two, out_grad, weight_one, weight_two):
    nx, ny, nz, _ = layer_input.shape
    core = lax.axis_index("gc").reshape(1).astype(jnp.int32)
    pre_one_f = pre_one.astype(F32)
    hidden = (pre_one_f * jnp.where(pre_one_f > 0, 1.0, slope_low)).astype(BF16)
    side = jnp.where(pre_one_f > 0, 1.0, -1.0).astype(BF16)
    slope_two = jnp.where(pre_two.astype(F32) > 0, 1.0, slope_low)
    g_two = (out_grad.astype(F32) * slope_two).astype(BF16)
    both = lax.optimization_barrier(jnp.concatenate([g_two, side], axis=0))
    g_two, side = both[:nx], both[nx:]
    lines = extend(g_two, side, core[0] == 1)

    taps_flops = 2 * 27 * C * C
    cells = nx * ny * nz
    pair_type = (nx + 2, ny // 2 + 2, PITCH, 3 * C)
    grads, pair_one = pl.pallas_call(
        functools.partial(main_kernel, float(cells_all) ** -0.5),
        out_shape=(
            jax.ShapeDtypeStruct((2, 27, C, C), BF16),
            jax.ShapeDtypeStruct(pair_type, BF16),
        ),
        in_specs=[pl.BlockSpec(memory_space=pltpu.SMEM)] + [vmem()] * 4,
        out_specs=(vmem(), vmem()),
        scratch_shapes=[
            pltpu.VMEM((nx + 4, ny + 4, PITCH, 3 * C), BF16),
            pltpu.VMEM(pair_type, BF16),
        ],
        compiler_params=pltpu.CompilerParams(vmem_limit_bytes=16 * 2**20),
        cost_estimate=pl.CostEstimate(
            flops=4 * cells * taps_flops, bytes_accessed=6 * 2**20, transcendentals=0
        ),
        name="kernel_gradients",
    )(
        core,
        lines,
        paired(hidden),
        paired(layer_input),
        weight_two.reshape(27, C, C),
    )
    mine = reduced(grads)
    other = lax.ppermute(mine, "gc", [(0, 1), (1, 0)])
    smem = pl.BlockSpec(memory_space=pltpu.SMEM)
    anywhere = pl.BlockSpec(memory_space=pl.ANY)
    total_type = jax.ShapeDtypeStruct((27, C, C), BF16)
    input_grad, grad_one, grad_two = pl.pallas_call(
        input_kernel,
        out_shape=(
            jax.ShapeDtypeStruct((nx, ny, nz, C), BF16),
            total_type,
            total_type,
        ),
        in_specs=[smem, vmem(), vmem(), anywhere],
        out_specs=(vmem(), anywhere, anywhere),
        scratch_shapes=[pltpu.SemaphoreType.DMA((9,))],
        compiler_params=pltpu.CompilerParams(vmem_limit_bytes=8 * 2**20),
        cost_estimate=pl.CostEstimate(
            flops=cells * taps_flops, bytes_accessed=2 * 2**20, transcendentals=0
        ),
        name="input_gradient",
    )(core, pair_one, weight_one.reshape(27, C, C), mine)
    grad_one, grad_two = pl.pallas_call(
        place_kernel,
        out_shape=(total_type, total_type),
        in_specs=[smem] + [anywhere] * 3,
        out_specs=(anywhere, anywhere),
        scratch_shapes=[pltpu.SemaphoreType.DMA((9,))],
        input_output_aliases={2: 0, 3: 1},
        compiler_params=pltpu.CompilerParams(vmem_limit_bytes=2**20),
        name="place_totals",
    )(core, other, grad_one, grad_two)
    shape = weight_one.shape
    return input_grad, grad_one.reshape(shape), grad_two.reshape(shape)


def solution(mesh):
    sizes = mesh.devices.shape
    cores, rows = 2, sizes[2] // 4
    devices = mesh.devices.reshape(sizes[0], sizes[1], 2, rows, cores)
    fine = Mesh(devices, ("gx", "gy", "gh", "gw", "gc"))
    split = P("gx", "gy", Z, None)

    def whole(*arrays):
        cells_all = 1
        for size in arrays[0].shape[:3]:
            cells_all *= size
        return jax.shard_map(
            functools.partial(on_device, cells_all),
            mesh=fine,
            in_specs=(split, split, split, split, P(), P()),
            out_specs=(split, P(), P()),
            check_vma=False,
        )(*arrays)

    return whole
```

```python
import functools

import jax
import jax.numpy as jnp
from jax import lax
from jax.experimental import pallas as pl
from jax.experimental.pallas import tpu as pltpu
from jax.sharding import Mesh
from jax.sharding import PartitionSpec as P
import numpy as np

slope_low = 0.3
Z = ("gh", "gw", "gc")
EVERY = ("gx", "gy", "gh", "gw", "gc")
C = 128
GROUP = 9
PITCH = 16
F32 = jnp.float32
BF16 = jnp.bfloat16


def exchange(up, down, axis):
    peers = lax.axis_size(axis)
    right = [(i, i + 1) for i in range(peers - 1)]
    left = [(i + 1, i) for i in range(peers - 1)]
    return lax.ppermute(up, axis, right), lax.ppermute(down, axis, left)


def pack(g, s):
    lines = g.shape[2]
    return jnp.concatenate(
        [g.reshape(-1, lines, C), s.reshape(-1, lines, C)], axis=0
    )


def unpack(rows, g_shape, s_shape):
    n = g_shape[0] * g_shape[1]
    return rows[:n].reshape(g_shape), rows[n:].reshape(s_shape)


def extend(g, s, upper):
    nx, ny, nz, _ = g.shape
    up, down = exchange(pack(g[-2:], s[-1:]), pack(g[:2], s[:1]), "gx")
    shapes = ((2, ny, nz, C), (1, ny, nz, C))
    (g_lo, s_lo), (g_hi, s_hi) = unpack(up, *shapes), unpack(down, *shapes)
    g = jnp.concatenate([g_lo, g, g_hi], axis=0)
    s = jnp.concatenate([s_lo, s, s_hi], axis=0)

    up, down = exchange(
        pack(g[:, -2:], s[:, -1:]), pack(g[:, :2], s[:, :1]), "gy"
    )
    shapes = ((nx + 4, 2, nz, C), (nx + 2, 1, nz, C))
    (g_lo, s_lo), (g_hi, s_hi) = unpack(up, *shapes), unpack(down, *shapes)
    g = jnp.concatenate([g_lo, g, g_hi], axis=1)
    s = jnp.concatenate([s_lo, s, s_hi], axis=1)

    lines = pack(g, s)
    last, first = lines[:, -2:], lines[:, :2]
    outer, inner = [], []
    for i in range(1, lax.axis_size(Z) - 1, 2):
        outer += [(i, i + 1), (i + 1, i)]
    for i in range(0, lax.axis_size(Z), 2):
        inner += [(i, i + 1), (i + 1, i)]
    far = lax.ppermute(jnp.where(upper, last, first), Z, outer)
    near = lax.ppermute(jnp.where(upper, first, last), Z, inner)
    lo, hi = jnp.where(upper, near, far), jnp.where(upper, far, near)
    rest = jnp.zeros((lines.shape[0], PITCH - nz - 4, C), BF16)
    return jnp.concatenate([lo, lines, hi, rest], axis=1)


def paired(cells):
    half = cells.shape[1] // 2
    return jnp.concatenate([cells[:, :half], cells[:, half:]], axis=2)


def moved(rows, by):
    n = rows.shape[0]
    return rows if by == 0 else pltpu.roll(rows, (n - by) % n, 0)


def wide_into(out_ref, cells):
    rows = cells.reshape(-1, C)
    for k in range(3):
        out_ref[..., k * C : (k + 1) * C] = (
            moved(rows, 1 - k).astype(BF16).reshape(cells.shape)
        )


def pairs_into(out_ref, cells, first):
    nx, ny = cells.shape[:2]
    rows = cells.reshape(-1, C)
    held = out_ref.shape[1]
    half = held - 2
    for k in range(3):
        lines = moved(rows, 3 - k).reshape(nx, ny, PITCH, C)[:, :, : PITCH // 2]
        low = lines[:, first : first + held]
        high = lines[:, first + half : first + half + held]
        out_ref[..., k * C : (k + 1) * C] = jnp.concatenate(
            [low, high], axis=2
        ).astype(BF16)


def taps():
    return [(a, b) for a in range(3) for b in range(3)]


def window(ref, tap, nx, ny):
    a, b = tap
    return ref[2 - a : 2 - a + nx, 2 - b : 2 - b + ny].reshape(nx * ny * PITCH, 3 * C)


def kernel_grads(act_t, ref, scale, out_ref, slot):
    nx, half = ref.shape[0] - 2, ref.shape[1] - 2
    for t, tap in enumerate(taps()):
        part = jnp.dot(
            act_t, window(ref, tap, nx, half), preferred_element_type=F32
        )
        part = (part * scale).astype(BF16)
        for k in range(3):
            out_ref[slot, t * 3 + k] = part[:, k * C : (k + 1) * C]


def input_grads(ref, w_ref, nx, ny):
    total = None
    for group in range(0, 9, GROUP):
        numbers = range(group, min(group + GROUP, 9))
        cells = [window(ref, taps()[t], nx, ny) for t in numbers]
        weights = [w_ref[3 * t + k] for t in numbers for k in range(3)]
        part = lax.dot_general(
            jnp.concatenate(cells, axis=1),
            jnp.concatenate(weights, axis=1),
            (((1,), (1,)), ((), ())),
            preferred_element_type=F32,
        )
        total = part if total is None else total + part
    return total


def two_planes(ref, w_ref, nx, ny):
    plane = ny * PITCH
    weights = [
        jnp.concatenate(
            [w_ref[(a * 3 + b) * 3 + k] for b in range(3) for k in range(3)], axis=1
        )
        for a in range(3)
    ]
    cells = [ref[1:, 2 - b : 2 - b + ny].reshape(-1, 3 * C) for b in range(3)]
    both = lax.dot_general(
        jnp.concatenate(cells, axis=1),
        jnp.concatenate(weights[:2], axis=0),
        (((1,), (1,)), ((), ())),
        preferred_element_type=F32,
    )
    cells = [window(ref, (2, b), nx, ny) for b in range(3)]
    rest = lax.dot_general(
        jnp.concatenate(cells, axis=1),
        weights[2],
        (((1,), (1,)), ((), ())),
        preferred_element_type=F32,
    )
    parts = []
    for x in range(nx):
        one, two = (x + 1) * plane, x * plane
        parts.append(both[one : one + plane, :C] + both[two : two + plane, C:])
    return jnp.concatenate(parts, axis=0) + rest


def main_kernel(
    scale, core_ref, lines_ref, hidden_ref, input_ref, w_ref, grads_ref, pair_one, wide, pair_two
):
    core = core_ref[0]
    nx, half = hidden_ref.shape[:2]
    ny = 2 * half
    split = (nx + 4) * (ny + 4)
    lines = lines_ref[:split].astype(F32).reshape(nx + 4, ny + 4, PITCH, C)
    wide_into(wide, lines)
    pairs_into(pair_two, lines[1 : nx + 3], 1)
    d_hidden = two_planes(wide, w_ref, nx + 2, ny + 2)
    side = lines_ref[split:].astype(F32).reshape(-1, C)
    slope = jnp.where(side > 0, 1.0, jnp.where(side < 0, slope_low, 0.0))
    g_one = (d_hidden * slope).astype(BF16).astype(F32)
    pairs_into(pair_one, g_one.reshape(nx + 2, ny + 2, PITCH, C), 0)
    hidden_t = hidden_ref[...].reshape(-1, C).T
    kernel_grads(hidden_t, pair_two, scale, grads_ref, 1 - core)
    input_t = input_ref[...].reshape(-1, C).T
    kernel_grads(input_t, pair_one, scale, grads_ref, core)


def input_kernel(core_ref, pair_ref, w_ref, mine_ref, out_ref, one_ref, two_ref, sems):
    def start(target):
        for copy in chunks(mine_ref, target, sems):
            copy.start()

    def finish(target):
        for copy in chunks(mine_ref, target, sems):
            copy.wait()

    on_core(core_ref, one_ref, two_ref, start)
    nx, ny, nz, _ = out_ref.shape
    half = ny // 2
    total = input_grads(pair_ref, w_ref, nx, half)
    total = total.reshape(nx, half, PITCH, C).astype(BF16)
    out_ref[:, :half] = total[:, :, :nz]
    out_ref[:, half:] = total[:, :, nz:]
    on_core(core_ref, one_ref, two_ref, finish)


def vmem():
    return pl.BlockSpec(memory_space=pltpu.VMEM)


def chunks(source, target, sems):
    step = target.shape[0] // sems.shape[0]
    copies = []
    for part in range(sems.shape[0]):
        rows = pl.ds(part * step, step)
        copies.append(
            pltpu.make_async_copy(source.at[rows], target.at[rows], sems.at[part])
        )
    return copies


def on_core(core_ref, first, second, act):
    for core, target in enumerate((first, second)):

        @pl.when(core_ref[0] == core)
        def _():
            act(target)


def place_kernel(core_ref, other_ref, _, __, one_ref, two_ref, sems):
    def run(target):
        copies = chunks(other_ref, target, sems)
        for copy in copies:
            copy.start()
        for copy in copies:
            copy.wait()

    on_core(core_ref, two_ref, one_ref, run)


def steps():
    sizes = [lax.axis_size(axis) for axis in EVERY]
    number = np.arange(np.prod(sizes)).reshape(sizes)
    nx, ny, nh, nw, _ = sizes

    def groups(devices, axes):
        size = np.prod([devices.shape[axis] for axis in axes])
        last = range(devices.ndim - len(axes), devices.ndim)
        return np.moveaxis(devices, axes, last).reshape(-1, size)

    zero = number[..., 0]
    one = number[..., 1].reshape(nx, ny // 2, 2, nh, nw // 2, 2)
    near = groups(zero, (0,)), groups(one, (2, 5))
    ring = groups(zero, (1, 2)), groups(one, (0, 1))
    far = groups(zero, (3,)), groups(one, (3, 4))
    return [np.concatenate(both).tolist() for both in (near, ring, far)]


def exchanged(pieces, groups):
    return lax.all_to_all(
        pieces, EVERY, 0, 0, axis_index_groups=groups, tiled=True
    )


def spread(rows, groups):
    return exchanged(
        jnp.broadcast_to(rows[None], (len(groups[0]),) + rows.shape), groups
    )


def scattered(rows, groups):
    return exchanged(rows.reshape(len(groups[0]), -1, C), groups)


def added(parts):
    return jnp.sum(parts.astype(F32), axis=0).astype(BF16)


def reduced(grads):
    got = lax.ppermute(grads[1], "gc", [(0, 1), (1, 0)])
    mine = (grads[0].astype(F32) + got.astype(F32)).astype(BF16)
    near, ring, far = steps()
    share = added(scattered(mine.reshape(-1, C), near))
    used = share.shape[0]
    rest = -used % (len(ring[0]) * PITCH)
    share = added(scattered(jnp.pad(share, ((0, rest), (0, 0))), ring))
    total = added(spread(share, far))
    total = spread(total, ring).reshape(-1, C)[:used]
    return spread(total, near).reshape(grads.shape[1:])


def on_device(cells_all, layer_input, pre_one, pre_two, out_grad, weight_one, weight_two):
    nx, ny, nz, _ = layer_input.shape
    core = lax.axis_index("gc").reshape(1).astype(jnp.int32)
    pre_one_f = pre_one.astype(F32)
    hidden = (pre_one_f * jnp.where(pre_one_f > 0, 1.0, slope_low)).astype(BF16)
    side = jnp.where(pre_one_f > 0, 1.0, -1.0).astype(BF16)
    slope_two = jnp.where(pre_two.astype(F32) > 0, 1.0, slope_low)
    g_two = (out_grad.astype(F32) * slope_two).astype(BF16)
    both = lax.optimization_barrier(jnp.concatenate([g_two, side], axis=0))
    g_two, side = both[:nx], both[nx:]
    lines = extend(g_two, side, core[0] == 1)

    taps_flops = 2 * 27 * C * C
    cells = nx * ny * nz
    pair_type = (nx + 2, ny // 2 + 2, PITCH, 3 * C)
    grads, pair_one = pl.pallas_call(
        functools.partial(main_kernel, float(cells_all) ** -0.5),
        out_shape=(
            jax.ShapeDtypeStruct((2, 27, C, C), BF16),
            jax.ShapeDtypeStruct(pair_type, BF16),
        ),
        in_specs=[pl.BlockSpec(memory_space=pltpu.SMEM)] + [vmem()] * 4,
        out_specs=(vmem(), vmem()),
        scratch_shapes=[
            pltpu.VMEM((nx + 4, ny + 4, PITCH, 3 * C), BF16),
            pltpu.VMEM(pair_type, BF16),
        ],
        compiler_params=pltpu.CompilerParams(vmem_limit_bytes=16 * 2**20),
        cost_estimate=pl.CostEstimate(
            flops=4 * cells * taps_flops, bytes_accessed=6 * 2**20, transcendentals=0
        ),
        name="kernel_gradients",
    )(
        core,
        lines,
        paired(hidden),
        paired(layer_input),
        weight_two.reshape(27, C, C),
    )
    mine = reduced(grads)
    other = lax.ppermute(mine, "gc", [(0, 1), (1, 0)])
    smem = pl.BlockSpec(memory_space=pltpu.SMEM)
    anywhere = pl.BlockSpec(memory_space=pl.ANY)
    total_type = jax.ShapeDtypeStruct((27, C, C), BF16)
    input_grad, grad_one, grad_two = pl.pallas_call(
        input_kernel,
        out_shape=(
            jax.ShapeDtypeStruct((nx, ny, nz, C), BF16),
            total_type,
            total_type,
        ),
        in_specs=[smem, vmem(), vmem(), anywhere],
        out_specs=(vmem(), anywhere, anywhere),
        scratch_shapes=[pltpu.SemaphoreType.DMA((9,))],
        compiler_params=pltpu.CompilerParams(vmem_limit_bytes=8 * 2**20),
        cost_estimate=pl.CostEstimate(
            flops=cells * taps_flops, bytes_accessed=2 * 2**20, transcendentals=0
        ),
        name="input_gradient",
    )(core, pair_one, weight_one.reshape(27, C, C), mine)
    grad_one, grad_two = pl.pallas_call(
        place_kernel,
        out_shape=(total_type, total_type),
        in_specs=[smem] + [anywhere] * 3,
        out_specs=(anywhere, anywhere),
        scratch_shapes=[pltpu.SemaphoreType.DMA((9,))],
        input_output_aliases={2: 0, 3: 1},
        compiler_params=pltpu.CompilerParams(vmem_limit_bytes=2**20),
        name="place_totals",
    )(core, other, grad_one, grad_two)
    shape = weight_one.shape
    return input_grad, grad_one.reshape(shape), grad_two.reshape(shape)


def solution(mesh):
    sizes = mesh.devices.shape
    cores, rows = 2, sizes[2] // 4
    devices = mesh.devices.reshape(sizes[0], sizes[1], 2, rows, cores)
    fine = Mesh(devices, ("gx", "gy", "gh", "gw", "gc"))
    split = P("gx", "gy", Z, None)

    def whole(*arrays):
        cells_all = 1
        for size in arrays[0].shape[:3]:
            cells_all *= size
        return jax.shard_map(
            functools.partial(on_device, cells_all),
            mesh=fine,
            in_specs=(split, split, split, split, P(), P()),
            out_specs=(split, P(), P()),
            check_vma=False,
        )(*arrays)

    return whole
```

```python
import functools

import jax
import jax.numpy as jnp
from jax import lax
from jax.experimental import pallas as pl
from jax.experimental.pallas import tpu as pltpu
from jax.sharding import Mesh
from jax.sharding import PartitionSpec as P
import numpy as np

slope_low = 0.3
Z = ("gh", "gw", "gc")
EVERY = ("gx", "gy", "gh", "gw", "gc")
C = 128
PITCH = 16
F32 = jnp.float32
BF16 = jnp.bfloat16


def exchange(up, down, axis):
    peers = lax.axis_size(axis)
    right = [(i, i + 1) for i in range(peers - 1)]
    left = [(i + 1, i) for i in range(peers - 1)]
    return lax.ppermute(up, axis, right), lax.ppermute(down, axis, left)


def pack(g, s):
    lines = g.shape[2]
    return jnp.concatenate(
        [g.reshape(-1, lines, C), s.reshape(-1, lines, C)], axis=0
    )


def unpack(rows, g_shape, s_shape):
    n = g_shape[0] * g_shape[1]
    return rows[:n].reshape(g_shape), rows[n:].reshape(s_shape)


def extend(g, s, upper):
    nx, ny, nz, _ = g.shape
    up, down = exchange(pack(g[-2:], s[-1:]), pack(g[:2], s[:1]), "gx")
    shapes = ((2, ny, nz, C), (1, ny, nz, C))
    (g_lo, s_lo), (g_hi, s_hi) = unpack(up, *shapes), unpack(down, *shapes)
    g = jnp.concatenate([g_lo, g, g_hi], axis=0)
    s = jnp.concatenate([s_lo, s, s_hi], axis=0)

    up, down = exchange(
        pack(g[:, -2:], s[:, -1:]), pack(g[:, :2], s[:, :1]), "gy"
    )
    shapes = ((nx + 4, 2, nz, C), (nx + 2, 1, nz, C))
    (g_lo, s_lo), (g_hi, s_hi) = unpack(up, *shapes), unpack(down, *shapes)
    g = jnp.concatenate([g_lo, g, g_hi], axis=1)
    s = jnp.concatenate([s_lo, s, s_hi], axis=1)

    lines = pack(g, s)
    last, first = lines[:, -2:], lines[:, :2]
    outer, inner = [], []
    for i in range(1, lax.axis_size(Z) - 1, 2):
        outer += [(i, i + 1), (i + 1, i)]
    for i in range(0, lax.axis_size(Z), 2):
        inner += [(i, i + 1), (i + 1, i)]
    far = lax.ppermute(jnp.where(upper, last, first), Z, outer)
    near = lax.ppermute(jnp.where(upper, first, last), Z, inner)
    lo, hi = jnp.where(upper, near, far), jnp.where(upper, far, near)
    rest = jnp.zeros((lines.shape[0], PITCH - nz - 4, C), BF16)
    return jnp.concatenate([lo, lines, hi, rest], axis=1)


def paired(cells):
    half = cells.shape[1] // 2
    return jnp.concatenate([cells[:, :half], cells[:, half:]], axis=2)


def moved(rows, by):
    n = rows.shape[0]
    return rows if by == 0 else pltpu.roll(rows, (n - by) % n, 0)


def wide_into(out_ref, cells):
    rows = cells.reshape(-1, C)
    for k in range(3):
        out_ref[..., k * C : (k + 1) * C] = (
            moved(rows, 1 - k).astype(BF16).reshape(cells.shape)
        )


def pairs_into(out_ref, cells, first):
    nx, ny = cells.shape[:2]
    rows = cells.reshape(-1, C)
    held = out_ref.shape[1]
    half = held - 2
    for k in range(3):
        lines = moved(rows, 3 - k).reshape(nx, ny, PITCH, C)[:, :, : PITCH // 2]
        low = lines[:, first : first + held]
        high = lines[:, first + half : first + half + held]
        out_ref[..., k * C : (k + 1) * C] = jnp.concatenate(
            [low, high], axis=2
        ).astype(BF16)


def taps():
    return [(a, b) for a in range(3) for b in range(3)]


def window(ref, tap, nx, ny):
    a, b = tap
    return ref[2 - a : 2 - a + nx, 2 - b : 2 - b + ny].reshape(nx * ny * PITCH, 3 * C)


def kernel_grads(act_t, ref, scale, out_ref, slot):
    nx, half = ref.shape[0] - 2, ref.shape[1] - 2
    for t, tap in enumerate(taps()):
        part = jnp.dot(
            act_t, window(ref, tap, nx, half), preferred_element_type=F32
        )
        part = (part * scale).astype(BF16)
        for k in range(3):
            out_ref[slot, t * 3 + k] = part[:, k * C : (k + 1) * C]


def two_planes(ref, w_ref, nx, ny):
    plane = ny * PITCH
    weights = [
        jnp.concatenate(
            [w_ref[(a * 3 + b) * 3 + k] for b in range(3) for k in range(3)], axis=1
        )
        for a in range(3)
    ]
    cells = [ref[1:, 2 - b : 2 - b + ny].reshape(-1, 3 * C) for b in range(3)]
    both = lax.dot_general(
        jnp.concatenate(cells, axis=1),
        jnp.concatenate(weights[:2], axis=0),
        (((1,), (1,)), ((), ())),
        preferred_element_type=F32,
    )
    cells = [window(ref, (2, b), nx, ny) for b in range(3)]
    rest = lax.dot_general(
        jnp.concatenate(cells, axis=1),
        weights[2],
        (((1,), (1,)), ((), ())),
        preferred_element_type=F32,
    )
    parts = []
    for x in range(nx):
        one, two = (x + 1) * plane, x * plane
        parts.append(both[one : one + plane, :C] + both[two : two + plane, C:])
    return jnp.concatenate(parts, axis=0) + rest


def main_kernel(
    scale, core_ref, lines_ref, hidden_ref, input_ref, w_ref, grads_ref, pair_one, wide, pair_two
):
    core = core_ref[0]
    nx, half = hidden_ref.shape[:2]
    ny = 2 * half
    split = (nx + 4) * (ny + 4)
    lines = lines_ref[:split].astype(F32).reshape(nx + 4, ny + 4, PITCH, C)
    wide_into(wide, lines)
    pairs_into(pair_two, lines[1 : nx + 3], 1)
    d_hidden = two_planes(wide, w_ref, nx + 2, ny + 2)
    side = lines_ref[split:].astype(F32).reshape(-1, C)
    slope = jnp.where(side > 0, 1.0, jnp.where(side < 0, slope_low, 0.0))
    g_one = (d_hidden * slope).astype(BF16).astype(F32)
    pairs_into(pair_one, g_one.reshape(nx + 2, ny + 2, PITCH, C), 0)
    hidden_t = hidden_ref[...].reshape(-1, C).T
    kernel_grads(hidden_t, pair_two, scale, grads_ref, 1 - core)
    input_t = input_ref[...].reshape(-1, C).T
    kernel_grads(input_t, pair_one, scale, grads_ref, core)


def input_kernel(core_ref, pair_ref, w_ref, mine_ref, out_ref, one_ref, two_ref, sems):
    def start(target):
        for copy in chunks(mine_ref, target, sems):
            copy.start()

    def finish(target):
        for copy in chunks(mine_ref, target, sems):
            copy.wait()

    on_core(core_ref, one_ref, two_ref, start)
    nx, ny, nz, _ = out_ref.shape
    half = ny // 2
    total = two_planes(pair_ref, w_ref, nx, half)
    total = total.reshape(nx, half, PITCH, C).astype(BF16)
    out_ref[:, :half] = total[:, :, :nz]
    out_ref[:, half:] = total[:, :, nz:]
    on_core(core_ref, one_ref, two_ref, finish)


def vmem():
    return pl.BlockSpec(memory_space=pltpu.VMEM)


def chunks(source, target, sems):
    step = target.shape[0] // sems.shape[0]
    copies = []
    for part in range(sems.shape[0]):
        rows = pl.ds(part * step, step)
        copies.append(
            pltpu.make_async_copy(source.at[rows], target.at[rows], sems.at[part])
        )
    return copies


def on_core(core_ref, first, second, act):
    for core, target in enumerate((first, second)):

        @pl.when(core_ref[0] == core)
        def _():
            act(target)


def place_kernel(core_ref, other_ref, _, __, one_ref, two_ref, sems):
    def run(target):
        copies = chunks(other_ref, target, sems)
        for copy in copies:
            copy.start()
        for copy in copies:
            copy.wait()

    on_core(core_ref, two_ref, one_ref, run)


def steps():
    sizes = [lax.axis_size(axis) for axis in EVERY]
    number = np.arange(np.prod(sizes)).reshape(sizes)
    nx, ny, nh, nw, _ = sizes

    def groups(devices, axes):
        size = np.prod([devices.shape[axis] for axis in axes])
        last = range(devices.ndim - len(axes), devices.ndim)
        return np.moveaxis(devices, axes, last).reshape(-1, size)

    zero = number[..., 0]
    one = number[..., 1].reshape(nx, ny // 2, 2, nh, nw // 2, 2)
    near = groups(zero, (0,)), groups(one, (2, 5))
    ring = groups(zero, (1, 2)), groups(one, (0, 1))
    far = groups(zero, (3,)), groups(one, (3, 4))
    return [np.concatenate(both).tolist() for both in (near, ring, far)]


def exchanged(pieces, groups):
    return lax.all_to_all(
        pieces, EVERY, 0, 0, axis_index_groups=groups, tiled=True
    )


def spread(rows, groups):
    return exchanged(
        jnp.broadcast_to(rows[None], (len(groups[0]),) + rows.shape), groups
    )


def scattered(rows, groups):
    return exchanged(rows.reshape(len(groups[0]), -1, C), groups)


def added(parts):
    return jnp.sum(parts.astype(F32), axis=0).astype(BF16)


def reduced(grads):
    got = lax.ppermute(grads[1], "gc", [(0, 1), (1, 0)])
    mine = (grads[0].astype(F32) + got.astype(F32)).astype(BF16)
    near, ring, far = steps()
    share = added(scattered(mine.reshape(-1, C), near))
    used = share.shape[0]
    rest = -used % (len(ring[0]) * PITCH)
    share = added(scattered(jnp.pad(share, ((0, rest), (0, 0))), ring))
    total = added(spread(share, far))
    total = spread(total, ring).reshape(-1, C)[:used]
    return spread(total, near).reshape(grads.shape[1:])


def on_device(cells_all, layer_input, pre_one, pre_two, out_grad, weight_one, weight_two):
    nx, ny, nz, _ = layer_input.shape
    core = lax.axis_index("gc").reshape(1).astype(jnp.int32)
    pre_one_f = pre_one.astype(F32)
    hidden = (pre_one_f * jnp.where(pre_one_f > 0, 1.0, slope_low)).astype(BF16)
    side = jnp.where(pre_one_f > 0, 1.0, -1.0).astype(BF16)
    slope_two = jnp.where(pre_two.astype(F32) > 0, 1.0, slope_low)
    g_two = (out_grad.astype(F32) * slope_two).astype(BF16)
    both = lax.optimization_barrier(jnp.concatenate([g_two, side], axis=0))
    g_two, side = both[:nx], both[nx:]
    lines = extend(g_two, side, core[0] == 1)

    taps_flops = 2 * 27 * C * C
    cells = nx * ny * nz
    pair_type = (nx + 2, ny // 2 + 2, PITCH, 3 * C)
    grads, pair_one = pl.pallas_call(
        functools.partial(main_kernel, float(cells_all) ** -0.5),
        out_shape=(
            jax.ShapeDtypeStruct((2, 27, C, C), BF16),
            jax.ShapeDtypeStruct(pair_type, BF16),
        ),
        in_specs=[pl.BlockSpec(memory_space=pltpu.SMEM)] + [vmem()] * 4,
        out_specs=(vmem(), vmem()),
        scratch_shapes=[
            pltpu.VMEM((nx + 4, ny + 4, PITCH, 3 * C), BF16),
            pltpu.VMEM(pair_type, BF16),
        ],
        compiler_params=pltpu.CompilerParams(vmem_limit_bytes=16 * 2**20),
        cost_estimate=pl.CostEstimate(
            flops=4 * cells * taps_flops, bytes_accessed=6 * 2**20, transcendentals=0
        ),
        name="kernel_gradients",
    )(
        core,
        lines,
        paired(hidden),
        paired(layer_input),
        weight_two.reshape(27, C, C),
    )
    mine = reduced(grads)
    other = lax.ppermute(mine, "gc", [(0, 1), (1, 0)])
    smem = pl.BlockSpec(memory_space=pltpu.SMEM)
    anywhere = pl.BlockSpec(memory_space=pl.ANY)
    total_type = jax.ShapeDtypeStruct((27, C, C), BF16)
    input_grad, grad_one, grad_two = pl.pallas_call(
        input_kernel,
        out_shape=(
            jax.ShapeDtypeStruct((nx, ny, nz, C), BF16),
            total_type,
            total_type,
        ),
        in_specs=[smem, vmem(), vmem(), anywhere],
        out_specs=(vmem(), anywhere, anywhere),
        scratch_shapes=[pltpu.SemaphoreType.DMA((9,))],
        compiler_params=pltpu.CompilerParams(vmem_limit_bytes=8 * 2**20),
        cost_estimate=pl.CostEstimate(
            flops=cells * taps_flops, bytes_accessed=2 * 2**20, transcendentals=0
        ),
        name="input_gradient",
    )(core, pair_one, weight_one.reshape(27, C, C), mine)
    grad_one, grad_two = pl.pallas_call(
        place_kernel,
        out_shape=(total_type, total_type),
        in_specs=[smem] + [anywhere] * 3,
        out_specs=(anywhere, anywhere),
        scratch_shapes=[pltpu.SemaphoreType.DMA((9,))],
        input_output_aliases={2: 0, 3: 1},
        compiler_params=pltpu.CompilerParams(vmem_limit_bytes=2**20),
        name="place_totals",
    )(core, other, grad_one, grad_two)
    shape = weight_one.shape
    return input_grad, grad_one.reshape(shape), grad_two.reshape(shape)


def solution(mesh):
    sizes = mesh.devices.shape
    cores, rows = 2, sizes[2] // 4
    devices = mesh.devices.reshape(sizes[0], sizes[1], 2, rows, cores)
    fine = Mesh(devices, ("gx", "gy", "gh", "gw", "gc"))
    split = P("gx", "gy", Z, None)

    def whole(*arrays):
        cells_all = 1
        for size in arrays[0].shape[:3]:
            cells_all *= size
        return jax.shard_map(
            functools.partial(on_device, cells_all),
            mesh=fine,
            in_specs=(split, split, split, split, P(), P()),
            out_specs=(split, P(), P()),
            check_vma=False,
        )(*arrays)

    return whole
```
